32 devices in a mesh: dp: 8 (over z, x), seq: 4 (over y, core).
Axes of the slice: x: 2, y: 2, z: 4, core: 2. Of those that a mesh axis runs over, the one named last changes fastest.
Arguments:
- tokens: bfloat16 [16384, 768], P(('dp', 'seq')), may hold values from -6 to 6
- cotangent: bfloat16 [16384, 768], P(('dp', 'seq')), may hold values from -6 to 6
- norm_gain: bfloat16 [2, 2, 768], P(None, None, ('dp', 'seq')), may hold values from 0.5 to 1.5
- norm_shift: bfloat16 [2, 2, 768], P(None, None, ('dp', 'seq')), may hold values from -1.796875 to 1.796875
- mixing_weight: bfloat16 [2, 768, 2304], P(None, ('dp', 'seq')), may hold values from -0.21875 to 0.21875
- mixing_bias: bfloat16 [2, 2, 768], P(None, None, ('dp', 'seq')), may hold values from -1.796875 to 1.796875
- output_weight: bfloat16 [2, 768, 768], P(None, ('dp', 'seq')), may hold values from -1.75 to 1.75
- output_bias: bfloat16 [2, 768], P(None, ('dp', 'seq')), may hold values from -1.796875 to 1.796875
- expand_weight: bfloat16 [2, 768, 3072], P(None, ('dp', 'seq')), may hold values from -0.21875 to 0.21875
- expand_bias: bfloat16 [2, 3072], P(None, ('dp', 'seq')), may hold values from -1.796875 to 1.796875
- reduce_weight: bfloat16 [2, 3072, 768], P(None, ('dp', 'seq')), may hold values from -0.109375 to 0.109375
- reduce_bias: bfloat16 [2, 768], P(None, ('dp', 'seq')), may hold values from -1.796875 to 1.796875
Outputs:
- out_tokens: bfloat16 [16384, 768], P(('dp', 'seq'))
- input_grad: float32 [16384, 768], P(('dp', 'seq'))
- norm_gain_grad: float32 [2, 2, 768], P(None, None, ('dp', 'seq'))
- norm_shift_grad: float32 [2, 2, 768], P(None, None, ('dp', 'seq'))
- mixing_weight_grad: float32 [2, 768, 2304], P(None, ('dp', 'seq'))
- mixing_bias_grad: float32 [2, 2, 768], P(None, None, ('dp', 'seq'))
- output_weight_grad: float32 [2, 768, 768], P(None, ('dp', 'seq'))
- output_bias_grad: float32 [2, 768], P(None, ('dp', 'seq'))
- expand_weight_grad: float32 [2, 768, 3072], P(None, ('dp', 'seq'))
- expand_bias_grad: float32 [2, 3072], P(None, ('dp', 'seq'))
- reduce_weight_grad: float32 [2, 3072, 768], P(None, ('dp', 'seq'))
- reduce_bias_grad: float32 [2, 768], P(None, ('dp', 'seq'))
The draws below stay inside these ranges and needn't reach their ends.
All inputs are finite; a program needn't handle non-finite values.
Results may differ from the reference program's by a relative error of at most 0.011.
Values may be sent and summed in bfloat16 or wider, within the bound.
A program may use at most 256 MiB of HBM per device.

```python
import jax
import jax.numpy as jnp
from jax import lax

D = 768
H = 12
HD = 64
FF = 3072
LAYERS = 2
SEQ_LEN = 2048
TOKENS = 16384
N_DP = 8


def block_levels(key, extent, split, smallest, high):
    def one(dim, shards_of):
        heights = jax.random.uniform(jax.random.fold_in(jax.random.fold_in(key, 6), dim), (shards_of,), jnp.float32, smallest / len(split), high / len(split))
        return jnp.repeat(jnp.exp(heights), extent[dim] // shards_of).reshape((-1,) + (1,) * (len(extent) - dim - 1))

    gain = one(*split[0])
    for cut in split[1:]:
        gain = gain * one(*cut)
    return gain


def noise(stream_key, extent, scale, reach, cuts=(), dtype=jnp.bfloat16):
    values = scale * jax.random.normal(stream_key, extent, jnp.float32)
    if cuts:
        values = values * block_levels(stream_key, extent, cuts, -0.22, 0.18)
    return jnp.clip(values, -reach, reach).astype(dtype)


def setup_inputs(seed: int = 0) -> dict:
    streams_of = jax.random.split(jax.random.key(seed), 13)
    return {
        "tokens": noise(streams_of[0], (TOKENS, D), 1.0, 6.0, ((0, 32),)),
        "cotangent": noise(streams_of[1], (TOKENS, D), 1.0, 6.0, ((0, 32),)),
        "norm_gain": jnp.clip(1.0 + 0.1 * jax.random.normal(streams_of[2], (LAYERS, 2, D), jnp.float32), 0.5, 1.5).astype(jnp.bfloat16),
        "norm_shift": noise(streams_of[3], (LAYERS, 2, D), 0.3, 1.796875, ((2, 32),)),
        "mixing_weight": noise(streams_of[4], (LAYERS, D, 3 * D), D ** -0.5, 0.21875, ((1, 32),)),
        "mixing_bias": noise(streams_of[5], (LAYERS, 2, D), 0.3, 1.796875, ((2, 32),)),
        "output_weight": noise(streams_of[6], (LAYERS, D, D), (D // 64) ** -0.5, 1.75, ((1, 32),)),
        "output_bias": noise(streams_of[7], (LAYERS, D), 0.3, 1.796875, ((1, 32),)),
        "expand_weight": noise(streams_of[8], (LAYERS, D, FF), D ** -0.5, 0.21875, ((1, 32),)),
        "expand_bias": noise(streams_of[9], (LAYERS, FF), 0.3, 1.796875, ((1, 32),)),
        "reduce_weight": noise(streams_of[10], (LAYERS, FF, D), FF ** -0.5, 0.109375, ((1, 32),)),
        "reduce_bias": noise(streams_of[11], (LAYERS, D), 0.3, 1.796875, ((1, 32),)),
    }


norm_epsilon = 1e-05

@jax.custom_vjp
def low(v):
    return lax.optimization_barrier(v.astype(jnp.bfloat16)).astype(jnp.float32)

@jax.custom_vjp
def low_back(v):
    return v

def low_keep(v):
    return (low(v), None)

def low_pass(kept, grad):
    return (grad,)

def back_keep(v):
    return (v, None)

def back_low(kept, grad):
    return (low(grad),)
low.defvjp(low_keep, low_pass)
low_back.defvjp(back_keep, back_low)

def layer_norm(values, gain_row, shift_row):
    center = values - lax.optimization_barrier(jnp.mean(values, axis=-1, keepdims=True))
    spread = lax.optimization_barrier(jnp.mean(center * center, axis=-1, keepdims=True))
    return center * lax.rsqrt(spread + norm_epsilon) * gain_row + shift_row

def matmul(left, right):
    return jnp.dot(left, right, precision=lax.Precision.HIGHEST)

def attention(mixed_rows):
    length = mixed_rows.shape[0]
    query = mixed_rows[:, :D].reshape(length, H, HD)
    keys = mixed_rows[:, D:2 * D].reshape(length, H, HD)
    values = mixed_rows[:, 2 * D:].reshape(length, H, HD)
    scores = jnp.einsum('qhd,khd->hqk', query, keys, precision=lax.Precision.HIGHEST) * HD ** (-0.5)
    scores = low_back(scores)
    position = jnp.arange(length)
    allowed = position[None, :] <= position[:, None]
    scores = jnp.where(allowed[None], scores, -1e+30)
    peak_score = lax.optimization_barrier(jnp.max(scores, axis=-1, keepdims=True))
    weights = jnp.exp(scores - peak_score)
    shares = low(weights / lax.optimization_barrier(jnp.sum(weights, axis=-1, keepdims=True)))
    attended = jnp.einsum('hqk,khd->qhd', shares, values, precision=lax.Precision.HIGHEST).reshape(length, D)
    return low_back(low(attended))

def run_sequence(hidden, params):
    norm_gain, norm_shift, mixing_weight, mixing_bias, output_weight, output_bias, expand_weight, expand_bias, reduce_weight, reduce_bias = params
    for layer_index in range(LAYERS):
        normed = low(layer_norm(hidden, norm_gain[layer_index, 0], norm_shift[layer_index, 0]))
        bias_row = jnp.concatenate([mixing_bias[layer_index, 0], jnp.zeros((D,), jnp.float32), mixing_bias[layer_index, 1]])
        mixed_rows = low_back(low(matmul(normed, mixing_weight[layer_index]) + bias_row))
        attended = attention(mixed_rows)
        middle = hidden + low_back(matmul(attended, output_weight[layer_index])) + output_bias[layer_index]
        normed_two = low(layer_norm(middle, norm_gain[layer_index, 1], norm_shift[layer_index, 1]))
        pre_gelu = low_back(matmul(normed_two, expand_weight[layer_index]) + expand_bias[layer_index])
        activated = low(jax.nn.gelu(pre_gelu, approximate=True))
        hidden = middle + low_back(matmul(activated, reduce_weight[layer_index])) + reduce_bias[layer_index]
    return hidden

def reference(tokens, cotangent, norm_gain, norm_shift, mixing_weight, mixing_bias, output_weight, output_bias, expand_weight, expand_bias, reduce_weight, reduce_bias):
    params = tuple((member.astype(jnp.float32) for member in (norm_gain, norm_shift, mixing_weight, mixing_bias, output_weight, output_bias, expand_weight, expand_bias, reduce_weight, reduce_bias)))

    def forward(hidden_all, weights_all):

        def one_sequence(rows_seq):
            return run_sequence(rows_seq, weights_all)
        sequences = hidden_all.reshape(N_DP, SEQ_LEN, D)
        outputs = lax.map(jax.checkpoint(one_sequence), sequences)
        return outputs.reshape(TOKENS, D)
    result, pullback = jax.vjp(forward, tokens.astype(jnp.float32), params)
    input_grad, grads = pullback(cotangent.astype(jnp.float32))
    return (result.astype(jnp.bfloat16), input_grad, grads[0], grads[1], grads[2], grads[3], grads[4], grads[5], grads[6], grads[7], grads[8], grads[9])
```

```python
import functools

import jax
import jax.numpy as jnp
from jax import lax
from jax.experimental import pallas as pl
from jax.experimental.pallas import tpu as pltpu
from jax.sharding import PartitionSpec as P

D = 768
HD = 64
LAYERS = 2
SCALE = HD ** (-0.5)
norm_epsilon = 1e-05


def layer_norm(values, gain_row, shift_row):
    center = values - jnp.mean(values, axis=-1, keepdims=True)
    spread = jnp.mean(center * center, axis=-1, keepdims=True)
    return center * lax.rsqrt(spread + norm_epsilon) * gain_row + shift_row


def gelu_tanh(values):
    return jax.nn.gelu(values, approximate=True)


def product(spec, left, right):
    return jnp.einsum(spec, left, right, preferred_element_type=jnp.float32)


def dot_f32(left, right, left_dim, right_dim):
    return lax.dot_general(
        left, right, (((left_dim,), (right_dim,)), ((), ())), preferred_element_type=jnp.float32
    )


def causal(scores):
    key_place = lax.broadcasted_iota(jnp.int32, scores.shape, 0)
    query_place = lax.broadcasted_iota(jnp.int32, scores.shape, 1)
    return jnp.where(key_place <= query_place, scores, -1e30)


def score_block(qkv_ref, query, i, j):
    scores = dot_f32(qkv_ref[j, 1, 0], query, 0, 0)
    return causal(scores) if i == j else scores


def forward_kernel(qkv_ref, out_ref, log_ref):
    parts = qkv_ref.shape[0]
    for i in range(parts):
        query = qkv_ref[i, 0, 0] * jnp.asarray(SCALE, jnp.bfloat16)
        scores = [score_block(qkv_ref, query, i, j) for j in range(i + 1)]
        peak = functools.reduce(
            jnp.maximum, [jnp.max(block, axis=0, keepdims=True) for block in scores]
        )
        total = 0.0
        summed = 0.0
        for j in range(i + 1):
            weights = jnp.exp(scores[j] - peak)
            total = total + jnp.sum(weights, axis=0, keepdims=True)
            summed = summed + dot_f32(qkv_ref[j, 2, 0], weights.astype(jnp.bfloat16), 1, 0)
        out_ref[i, 0] = (summed / total).astype(jnp.bfloat16)
        log_ref[0, i] = peak + jnp.log(total)


def backward_kernel(qkv_ref, grad_ref, log_ref, out_ref, key_acc, value_acc):
    parts = qkv_ref.shape[0]
    for i in range(parts):
        query = qkv_ref[i, 0, 0] * jnp.asarray(SCALE, jnp.bfloat16)
        grad = grad_ref[i, 0]
        log_total = log_ref[0, i]
        shares = []
        share_grads = []
        inner = 0.0
        for j in range(i + 1):
            share = jnp.exp(score_block(qkv_ref, query, i, j) - log_total)
            share_grad = dot_f32(qkv_ref[j, 2, 0], grad, 0, 0)
            inner = inner + jnp.sum(share * share_grad, axis=0, keepdims=True)
            shares.append(share)
            share_grads.append(share_grad)
        query_grad = 0.0
        for j in range(i + 1):
            score_grad = (shares[j] * (share_grads[j] - inner)).astype(jnp.bfloat16)
            value_part = dot_f32(grad, shares[j].astype(jnp.bfloat16), 1, 1)
            key_part = dot_f32(query, score_grad, 1, 1)
            query_grad = query_grad + dot_f32(qkv_ref[j, 1, 0], score_grad, 1, 0)
            if i == j:
                key_acc[j] = key_part
                value_acc[j] = value_part
            else:
                key_acc[j] += key_part
                value_acc[j] += value_part
        out_ref[i, 0, 0] = (query_grad * SCALE).astype(jnp.bfloat16)
    for j in range(parts):
        out_ref[j, 1, 0] = key_acc[j].astype(jnp.bfloat16)
        out_ref[j, 2, 0] = value_acc[j].astype(jnp.bfloat16)


def attention_cost(qkv, products):
    parts, _, heads, width, length = qkv.shape
    pairs = parts * (parts + 1) // 2 * length * length * heads
    return pl.CostEstimate(
        flops=4 * products * pairs * width,
        transcendentals=pairs,
        bytes_accessed=2 * qkv.size * 2,
    )


def attend_forward(qkv):
    parts, _, heads, width, length = qkv.shape
    return pl.pallas_call(
        forward_kernel,
        grid=(heads,),
        in_specs=[pl.BlockSpec((parts, 3, 1, width, length), lambda h: (0, 0, h, 0, 0))],
        out_specs=[
            pl.BlockSpec((parts, 1, width, length), lambda h: (0, h, 0, 0)),
            pl.BlockSpec((1, parts, 1, length), lambda h: (h, 0, 0, 0)),
        ],
        out_shape=[
            jax.ShapeDtypeStruct((parts, heads, width, length), jnp.bfloat16),
            jax.ShapeDtypeStruct((heads, parts, 1, length), jnp.float32),
        ],
        compiler_params=pltpu.CompilerParams(vmem_limit_bytes=40 * 2**20),
        cost_estimate=attention_cost(qkv, 2),
    )(qkv)


def attend_backward(qkv, grad, log_total):
    parts, _, heads, width, length = qkv.shape
    qkv_spec = pl.BlockSpec((parts, 3, 1, width, length), lambda h: (0, 0, h, 0, 0))
    return pl.pallas_call(
        backward_kernel,
        grid=(heads,),
        in_specs=[
            qkv_spec,
            pl.BlockSpec((parts, 1, width, length), lambda h: (0, h, 0, 0)),
            pl.BlockSpec((1, parts, 1, length), lambda h: (h, 0, 0, 0)),
        ],
        out_specs=qkv_spec,
        out_shape=jax.ShapeDtypeStruct(qkv.shape, jnp.bfloat16),
        scratch_shapes=[
            pltpu.VMEM((parts, width, length), jnp.float32),
            pltpu.VMEM((parts, width, length), jnp.float32),
        ],
        compiler_params=pltpu.CompilerParams(vmem_limit_bytes=40 * 2**20),
        cost_estimate=attention_cost(qkv, 5),
    )(qkv, grad, log_total)


def place_bits():
    dp_bits = lax.axis_size("dp").bit_length() - 1
    seq_bits = lax.axis_size("seq").bit_length() - 1
    bits = [("dp", dp_bits - 1 - n) for n in range(dp_bits)]
    return bits + [("seq", seq_bits - 1 - n) for n in range(seq_bits)]


def my_bit(bit):
    return lax.rem(lax.axis_index(bit[0]) // (1 << bit[1]), 2)


def exchange(values, bit):
    name, place = bit
    count = lax.axis_size(name)
    return lax.ppermute(values, name, [(i, i ^ (1 << place)) for i in range(count)])


def sum_order(style):
    bits = place_bits()
    core, other, spread = bits[-1], bits[-2], bits[:-2][::-1]
    if style == 0:
        rest = [other] + spread
    elif style == 1:
        rest = spread + [other]
    else:
        rest = spread[1:2] + [other] + spread[:1] + spread[2:]
    return [core] + rest


def gather(piece, style):
    bits = place_bits()
    have = []
    block = piece
    for bit in reversed(sum_order(style)):
        axis = sum(1 for other in have if bits.index(other) < bits.index(bit))
        received = exchange(block, bit)
        shape = block.shape[:axis] + (2,) + block.shape[axis:]
        twice = jnp.broadcast_to(jnp.expand_dims(block, axis), shape)
        block = lax.dynamic_update_slice_in_dim(
            twice, jnp.expand_dims(received, axis), 1 - my_bit(bit), axis
        )
        have.append(bit)
    rows = piece.shape[0] * 2 ** len(bits)
    return block.reshape((rows,) + piece.shape[1:])


def scatter_sum(whole, style, sent=jnp.bfloat16):
    bits = place_bits()
    rows = whole.shape[0] >> len(bits)
    block = whole.reshape((2,) * len(bits) + (rows,) + whole.shape[1:])
    left = list(bits)
    for bit in sum_order(style):
        axis = left.index(bit)
        at = my_bit(bit)
        away = lax.dynamic_index_in_dim(block, 1 - at, axis, keepdims=False).astype(sent)
        kept = lax.dynamic_index_in_dim(block, at, axis, keepdims=False)
        block = kept + exchange(away, bit).astype(jnp.float32)
        left.remove(bit)
    return block


SMALL = (8, 128)


def body(
    tokens,
    cotangent,
    norm_gain,
    norm_shift,
    mixing_weight,
    mixing_bias,
    output_weight,
    output_bias,
    expand_weight,
    expand_bias,
    reduce_weight,
    reduce_bias,
):
    parts = lax.axis_size("seq")
    local_rows = tokens.shape[0]
    head_group = D // parts
    heads = head_group // HD

    small_members = (norm_gain, norm_shift, mixing_bias, output_bias, expand_bias, reduce_bias)
    flat = jnp.concatenate([member.reshape(-1) for member in small_members])
    slots = SMALL[0] * SMALL[1] * (-(-flat.shape[0] // (SMALL[0] * SMALL[1])))
    flat = jnp.pad(flat, (0, slots - flat.shape[0]))
    small = gather(flat.reshape(-1, 128), 0)
    small = small.reshape(-1, slots).astype(jnp.float32)
    devices = small.shape[0]
    small_rows = []
    start = 0
    for member in small_members:
        piece = small[:, start : start + member.size].reshape((devices,) + member.shape)
        start += member.size
        small_rows.append(jnp.moveaxis(piece, 0, -2).reshape(member.shape[:-1] + (-1,)))
    gains_all, shifts_all, mix_bias_all, out_bias_all, exp_bias_all, red_bias_all = small_rows

    def mixing_thirds(piece):
        return [gather(piece[:, n * D : (n + 1) * D], n) for n in range(3)]

    def later_weights(output_piece, expand_piece, reduce_piece):
        half = expand_piece.shape[1] // 2
        return (
            gather(output_piece, 2),
            (gather(expand_piece[:, :half], 0), gather(expand_piece[:, half:], 1)),
            gather(reduce_piece, 1),
        )

    mixing_first = mixing_thirds(mixing_weight[0])
    out_piece, exp_piece, red_piece, mixing_first = lax.optimization_barrier(
        (output_weight[0], expand_weight[0], reduce_weight[0], mixing_first)
    )
    first_rest = later_weights(out_piece, exp_piece, red_piece)
    mix_piece, out_piece, exp_piece, red_piece, first_rest = lax.optimization_barrier(
        (mixing_weight[1], output_weight[1], expand_weight[1], reduce_weight[1], first_rest)
    )
    mixing_second = mixing_thirds(mix_piece)
    second_rest = later_weights(out_piece, exp_piece, red_piece)
    weights = [(mixing_first,) + first_rest, (mixing_second,) + second_rest]

    hidden = tokens.astype(jnp.float32)
    saved = []
    for layer_index in range(LAYERS):
        mixing, output, expand, reduce = weights[layer_index]
        gains = gains_all[layer_index]
        shifts = shifts_all[layer_index]
        normed = layer_norm(hidden, gains[0], shifts[0]).astype(jnp.bfloat16)
        thirds = []
        for n in range(3):
            third = product("td,dc->ct", normed, mixing[n])
            if n != 1:
                third = third + mix_bias_all[layer_index, n // 2][:, None]
            thirds.append(third.astype(jnp.bfloat16).reshape(parts, heads, HD, local_rows))
        packed = lax.all_to_all(
            jnp.stack(thirds, axis=1), "seq", split_axis=0, concat_axis=0, tiled=True
        )
        attended, log_totals = attend_forward(packed)
        merged = lax.all_to_all(
            attended, "seq", split_axis=0, concat_axis=0, tiled=True
        ).reshape(D, local_rows)
        middle = hidden + (product("it,id->td", merged, output) + out_bias_all[layer_index])
        normed_two = layer_norm(middle, gains[1], shifts[1]).astype(jnp.bfloat16)
        pre_gelu = (
            jnp.concatenate([product("td,df->tf", normed_two, half) for half in expand], axis=1)
            + exp_bias_all[layer_index]
        )
        activated = gelu_tanh(pre_gelu).astype(jnp.bfloat16)
        saved.append((hidden, normed, packed, log_totals, merged, middle, normed_two, pre_gelu, activated))
        hidden = middle + (product("tf,fd->td", activated, reduce) + red_bias_all[layer_index])
    out_tokens = hidden.astype(jnp.bfloat16)

    running_grad = cotangent.astype(jnp.float32)
    large = [None] * LAYERS
    small_grads = [None] * LAYERS
    for layer_index in reversed(range(LAYERS)):
        layer_input, normed, packed, log_totals, merged, middle, normed_two, pre_gelu, activated = saved[
            layer_index
        ]
        mixing, output, expand, reduce = weights[layer_index]
        gains = gains_all[layer_index]
        shifts = shifts_all[layer_index]
        reduce_bias_grad = jnp.sum(running_grad, axis=0)
        grad_low = running_grad.astype(jnp.bfloat16)
        reduce_shard = scatter_sum(product("tf,td->fd", activated, grad_low), 1)
        act_grad = product("td,fd->tf", grad_low, reduce)
        unused_value, gelu_pull = jax.vjp(gelu_tanh, pre_gelu)
        pre_grad = gelu_pull(act_grad)[0].astype(jnp.bfloat16)
        expand_bias_grad = jnp.sum(pre_grad.astype(jnp.float32), axis=0)
        half = pre_grad.shape[1] // 2
        halves = (pre_grad[:, :half], pre_grad[:, half:])
        expand_shard = jnp.concatenate(
            [scatter_sum(product("td,tf->df", normed_two, halves[n]), 2 * n) for n in range(2)], axis=1
        )
        second_in = product("tf,df->td", halves[0], expand[0]) + product(
            "tf,df->td", halves[1], expand[1]
        )
        unused_norm, norm_pull = jax.vjp(layer_norm, middle, gains[1], shifts[1])
        middle_grad, gain_two, shift_two = norm_pull(second_in)
        running_grad = running_grad + middle_grad
        output_bias_grad = jnp.sum(running_grad, axis=0)
        out_low = running_grad.astype(jnp.bfloat16)
        output_shard = scatter_sum(product("it,td->id", merged, out_low), 2)
        merged_grad = product("td,id->it", out_low, output).astype(jnp.bfloat16)
        head_grad = lax.all_to_all(
            merged_grad.reshape(parts, heads, HD, local_rows),
            "seq",
            split_axis=0,
            concat_axis=0,
            tiled=True,
        )
        packed_grad = attend_backward(packed, head_grad, log_totals)
        mixed_grad = lax.all_to_all(
            packed_grad, "seq", split_axis=0, concat_axis=0, tiled=True
        )
        grad_thirds = [mixed_grad[:, n].reshape(D, local_rows) for n in range(3)]
        mixing_shard = jnp.concatenate(
            [scatter_sum(product("td,ct->dc", normed, grad_thirds[n]), n) for n in range(3)], axis=1
        )
        mixing_bias_grad = jnp.stack(
            [jnp.sum(grad_thirds[n].astype(jnp.float32), axis=1) for n in (0, 2)]
        )
        first_in = sum(product("ct,dc->td", grad_thirds[n], mixing[n]) for n in range(3))
        unused_first, first_pull = jax.vjp(layer_norm, layer_input, gains[0], shifts[0])
        input_part, gain_one, shift_one = first_pull(first_in)
        running_grad = running_grad + input_part
        large[layer_index] = (mixing_shard, output_shard, expand_shard, reduce_shard)
        small_grads[layer_index] = (
            jnp.stack([gain_one, gain_two]),
            jnp.stack([shift_one, shift_two]),
            mixing_bias_grad,
            output_bias_grad,
            expand_bias_grad,
            reduce_bias_grad,
        )

    rows = []
    for n, member in enumerate(small_members):
        both = jnp.stack([small_grads[index][n] for index in range(LAYERS)])
        both = both.reshape(both.shape[:-1] + (devices, -1))
        rows.append(jnp.moveaxis(both, -2, 0).reshape(devices, -1))
    packed_rows = jnp.concatenate(rows, axis=1)
    packed_rows = jnp.pad(packed_rows, ((0, 0), (0, slots - packed_rows.shape[1])))
    sums = scatter_sum(packed_rows.reshape(-1, 128), 0, jnp.float32).reshape(-1)
    shards = []
    start = 0
    for member in small_members:
        shards.append(sums[start : start + member.size].reshape(member.shape))
        start += member.size
    gain_out, shift_out, mix_bias_out, out_bias_out, exp_bias_out, red_bias_out = shards
    mixing_out, output_out, expand_out, reduce_out = (
        jnp.stack([large[index][n] for index in range(LAYERS)]) for n in range(4)
    )
    return (
        out_tokens,
        running_grad,
        gain_out,
        shift_out,
        mixing_out,
        mix_bias_out,
        output_out,
        out_bias_out,
        expand_out,
        exp_bias_out,
        reduce_out,
        red_bias_out,
    )


def solution(mesh):
    return jax.shard_map(
        body,
        mesh=mesh,
        in_specs=(
            P(("dp", "seq"), None),
            P(("dp", "seq"), None),
            P(None, None, ("dp", "seq")),
            P(None, None, ("dp", "seq")),
            P(None, ("dp", "seq"), None),
            P(None, None, ("dp", "seq")),
            P(None, ("dp", "seq"), None),
            P(None, ("dp", "seq")),
            P(None, ("dp", "seq"), None),
            P(None, ("dp", "seq")),
            P(None, ("dp", "seq"), None),
            P(None, ("dp", "seq")),
        ),
        out_specs=(
            P(("dp", "seq"), None),
            P(("dp", "seq"), None),
            P(None, None, ("dp", "seq")),
            P(None, None, ("dp", "seq")),
            P(None, ("dp", "seq"), None),
            P(None, None, ("dp", "seq")),
            P(None, ("dp", "seq"), None),
            P(None, ("dp", "seq")),
            P(None, ("dp", "seq"), None),
            P(None, ("dp", "seq")),
            P(None, ("dp", "seq"), None),
            P(None, ("dp", "seq")),
        ),
        check_vma=False,
    )
```

```python
import functools

import jax
import jax.numpy as jnp
from jax import lax
from jax.experimental import pallas as pl
from jax.experimental.pallas import tpu as pltpu
from jax.sharding import PartitionSpec as P

D = 768
HD = 64
LAYERS = 2
SCALE = HD ** (-0.5)
norm_epsilon = 1e-05


def layer_norm(values, gain_row, shift_row):
    center = values - jnp.mean(values, axis=-1, keepdims=True)
    spread = jnp.mean(center * center, axis=-1, keepdims=True)
    return center * lax.rsqrt(spread + norm_epsilon) * gain_row + shift_row


def gelu_tanh(values):
    return jax.nn.gelu(values, approximate=True)


def product(spec, left, right):
    return jnp.einsum(spec, left, right, preferred_element_type=jnp.float32)


def dot_f32(left, right, left_dim, right_dim):
    return lax.dot_general(
        left, right, (((left_dim,), (right_dim,)), ((), ())), preferred_element_type=jnp.float32
    )


def causal(scores):
    key_place = lax.broadcasted_iota(jnp.int32, scores.shape, 0)
    query_place = lax.broadcasted_iota(jnp.int32, scores.shape, 1)
    return jnp.where(key_place <= query_place, scores, -1e30)


def score_block(qkv_ref, query, i, j):
    scores = dot_f32(qkv_ref[j, 1, 0], query, 0, 0)
    return causal(scores) if i == j else scores


def forward_kernel(qkv_ref, out_ref, log_ref):
    parts = qkv_ref.shape[0]
    for i in range(parts):
        query = qkv_ref[i, 0, 0] * jnp.asarray(SCALE, jnp.bfloat16)
        scores = [score_block(qkv_ref, query, i, j) for j in range(i + 1)]
        peak = functools.reduce(
            jnp.maximum, [jnp.max(block, axis=0, keepdims=True) for block in scores]
        )
        total = 0.0
        summed = 0.0
        for j in range(i + 1):
            weights = jnp.exp(scores[j] - peak)
            total = total + jnp.sum(weights, axis=0, keepdims=True)
            summed = summed + dot_f32(qkv_ref[j, 2, 0], weights.astype(jnp.bfloat16), 1, 0)
        out_ref[i, 0] = (summed / total).astype(jnp.bfloat16)
        log_ref[0, i] = peak + jnp.log(total)


def backward_kernel(qkv_ref, grad_ref, log_ref, out_ref, key_acc, value_acc):
    parts = qkv_ref.shape[0]
    for i in range(parts):
        query = qkv_ref[i, 0, 0] * jnp.asarray(SCALE, jnp.bfloat16)
        grad = grad_ref[i, 0]
        log_total = log_ref[0, i]
        shares = []
        share_grads = []
        inner = 0.0
        for j in range(i + 1):
            share = jnp.exp(score_block(qkv_ref, query, i, j) - log_total)
            share_grad = dot_f32(qkv_ref[j, 2, 0], grad, 0, 0)
            inner = inner + jnp.sum(share * share_grad, axis=0, keepdims=True)
            shares.append(share)
            share_grads.append(share_grad)
        query_grad = 0.0
        for j in range(i + 1):
            score_grad = (shares[j] * (share_grads[j] - inner)).astype(jnp.bfloat16)
            value_part = dot_f32(grad, shares[j].astype(jnp.bfloat16), 1, 1)
            key_part = dot_f32(query, score_grad, 1, 1)
            query_grad = query_grad + dot_f32(qkv_ref[j, 1, 0], score_grad, 1, 0)
            if i == j:
                key_acc[j] = key_part
                value_acc[j] = value_part
            else:
                key_acc[j] += key_part
                value_acc[j] += value_part
        out_ref[i, 0, 0] = (query_grad * SCALE).astype(jnp.bfloat16)
    for j in range(parts):
        out_ref[j, 1, 0] = key_acc[j].astype(jnp.bfloat16)
        out_ref[j, 2, 0] = value_acc[j].astype(jnp.bfloat16)


def attention_cost(qkv, products):
    parts, _, heads, width, length = qkv.shape
    pairs = parts * (parts + 1) // 2 * length * length * heads
    return pl.CostEstimate(
        flops=4 * products * pairs * width,
        transcendentals=pairs,
        bytes_accessed=2 * qkv.size * 2,
    )


def attend_forward(qkv):
    parts, _, heads, width, length = qkv.shape
    return pl.pallas_call(
        forward_kernel,
        grid=(heads,),
        in_specs=[pl.BlockSpec((parts, 3, 1, width, length), lambda h: (0, 0, h, 0, 0))],
        out_specs=[
            pl.BlockSpec((parts, 1, width, length), lambda h: (0, h, 0, 0)),
            pl.BlockSpec((1, parts, 1, length), lambda h: (h, 0, 0, 0)),
        ],
        out_shape=[
            jax.ShapeDtypeStruct((parts, heads, width, length), jnp.bfloat16),
            jax.ShapeDtypeStruct((heads, parts, 1, length), jnp.float32),
        ],
        compiler_params=pltpu.CompilerParams(vmem_limit_bytes=40 * 2**20),
        cost_estimate=attention_cost(qkv, 2),
    )(qkv)


def attend_backward(qkv, grad, log_total):
    parts, _, heads, width, length = qkv.shape
    qkv_spec = pl.BlockSpec((parts, 3, 1, width, length), lambda h: (0, 0, h, 0, 0))
    return pl.pallas_call(
        backward_kernel,
        grid=(heads,),
        in_specs=[
            qkv_spec,
            pl.BlockSpec((parts, 1, width, length), lambda h: (0, h, 0, 0)),
            pl.BlockSpec((1, parts, 1, length), lambda h: (h, 0, 0, 0)),
        ],
        out_specs=qkv_spec,
        out_shape=jax.ShapeDtypeStruct(qkv.shape, jnp.bfloat16),
        scratch_shapes=[
            pltpu.VMEM((parts, width, length), jnp.float32),
            pltpu.VMEM((parts, width, length), jnp.float32),
        ],
        compiler_params=pltpu.CompilerParams(vmem_limit_bytes=40 * 2**20),
        cost_estimate=attention_cost(qkv, 5),
    )(qkv, grad, log_total)


def place_bits():
    dp_bits = lax.axis_size("dp").bit_length() - 1
    seq_bits = lax.axis_size("seq").bit_length() - 1
    bits = [("dp", dp_bits - 1 - n) for n in range(dp_bits)]
    return bits + [("seq", seq_bits - 1 - n) for n in range(seq_bits)]


def my_bit(bit):
    return lax.rem(lax.axis_index(bit[0]) // (1 << bit[1]), 2)


def exchange(values, bit):
    name, place = bit
    count = lax.axis_size(name)
    return lax.ppermute(values, name, [(i, i ^ (1 << place)) for i in range(count)])


def sum_order(style):
    bits = place_bits()
    core, other, spread = bits[-1], bits[-2], bits[:-2][::-1]
    if style == 0:
        rest = [other] + spread
    elif style == 1:
        rest = spread + [other]
    else:
        rest = spread[1:2] + [other] + spread[:1] + spread[2:]
    return [core] + rest


class Gather:
    def __init__(self, piece, style):
        self.bits = place_bits()
        self.order = list(reversed(sum_order(style)))
        self.have = []
        self.block = piece
        self.tail = (piece.shape[0] << len(self.bits),) + piece.shape[1:]

    def step(self):
        if len(self.have) == len(self.order):
            return
        bit = self.order[len(self.have)]
        axis = sum(1 for other in self.have if self.bits.index(other) < self.bits.index(bit))
        received = exchange(self.block, bit)
        shape = self.block.shape[:axis] + (2,) + self.block.shape[axis:]
        twice = jnp.broadcast_to(jnp.expand_dims(self.block, axis), shape)
        self.block = lax.dynamic_update_slice_in_dim(
            twice, jnp.expand_dims(received, axis), 1 - my_bit(bit), axis
        )
        self.have.append(bit)

    def result(self):
        return self.block.reshape(self.tail)


class ScatterSum:
    def __init__(self, whole, style, sent=jnp.bfloat16):
        bits = place_bits()
        rows = whole.shape[0] >> len(bits)
        self.block = whole.reshape((2,) * len(bits) + (rows,) + whole.shape[1:])
        self.left = list(bits)
        self.order = sum_order(style)
        self.sent = sent

    def step(self):
        if not self.left:
            return
        bit = self.order[-len(self.left)]
        axis = self.left.index(bit)
        at = my_bit(bit)
        away = lax.dynamic_index_in_dim(self.block, 1 - at, axis, keepdims=False)
        kept = lax.dynamic_index_in_dim(self.block, at, axis, keepdims=False)
        self.block = kept + exchange(away.astype(self.sent), bit).astype(jnp.float32)
        self.left.remove(bit)

    def result(self):
        return self.block


def advance(movers, steps):
    for _ in range(steps):
        for mover in movers:
            mover.step()


def finish(movers):
    advance(movers, len(place_bits()))
    return [mover.result() for mover in movers]


def hold(value, movers):
    value, blocks = lax.optimization_barrier((value, [mover.block for mover in movers]))
    for mover, block in zip(movers, blocks):
        mover.block = block
    return value


SMALL = (8, 128)


def body(
    tokens,
    cotangent,
    norm_gain,
    norm_shift,
    mixing_weight,
    mixing_bias,
    output_weight,
    output_bias,
    expand_weight,
    expand_bias,
    reduce_weight,
    reduce_bias,
):
    parts = lax.axis_size("seq")
    local_rows = tokens.shape[0]
    head_group = D // parts
    heads = head_group // HD

    def mixing_gathers(piece, cuts):
        width = piece.shape[1] // cuts
        return [Gather(piece[:, n * width : (n + 1) * width], n) for n in range(cuts)]

    def later_weights(output_piece, expand_piece, reduce_piece):
        rows = output_piece.shape[0]
        flat = jnp.concatenate([output_piece, expand_piece, reduce_piece.reshape(rows, -1)], axis=1)
        width = flat.shape[1] // 3
        return [Gather(flat[:, n * width : (n + 1) * width], n) for n in range(3)]

    def split_weights(chunks):
        half = expand_weight.shape[2] // 2
        first, second, third = chunks
        expand = (first[:, D:], second[:, :half])
        reduce = jnp.concatenate([second[:, half:], third], axis=1).reshape(-1, D)
        return first[:, :D], expand, reduce

    small_members = (norm_gain, norm_shift, mixing_bias, output_bias, expand_bias, reduce_bias)
    flat = jnp.concatenate([member.reshape(-1) for member in small_members])
    slots = SMALL[0] * SMALL[1] * (-(-flat.shape[0] // (SMALL[0] * SMALL[1])))
    flat = jnp.pad(flat, (0, slots - flat.shape[0]))
    small_mover = Gather(flat.reshape(-1, 128), 0)
    mixing_movers = mixing_gathers(mixing_weight[0], 3)
    rest_movers = later_weights(output_weight[0], expand_weight[0], reduce_weight[0])
    small = finish([small_mover] + mixing_movers)[0]
    small = small.reshape(-1, slots).astype(jnp.float32)
    devices = small.shape[0]
    small_rows = []
    start = 0
    for member in small_members:
        piece = small[:, start : start + member.size].reshape((devices,) + member.shape)
        start += member.size
        small_rows.append(jnp.moveaxis(piece, 0, -2).reshape(member.shape[:-1] + (-1,)))
    gains_all, shifts_all, mix_bias_all, out_bias_all, exp_bias_all, red_bias_all = small_rows

    hidden = tokens.astype(jnp.float32)
    saved = []
    weights = []
    for layer_index in range(LAYERS):
        mixing = finish(mixing_movers)
        if len(mixing) == 1:
            mixing = [mixing[0][:, n * D : (n + 1) * D] for n in range(3)]
        gains = gains_all[layer_index]
        shifts = shifts_all[layer_index]
        mixing = hold(mixing, rest_movers)
        advance(rest_movers, 2)
        normed = layer_norm(hidden, gains[0], shifts[0]).astype(jnp.bfloat16)
        thirds = []
        for n in range(3):
            third = product("td,dc->ct", normed, mixing[n])
            if n != 1:
                third = third + mix_bias_all[layer_index, n // 2][:, None]
            thirds.append(third.astype(jnp.bfloat16).reshape(parts, heads, HD, local_rows))
        packed = lax.all_to_all(
            jnp.stack(thirds, axis=1), "seq", split_axis=0, concat_axis=0, tiled=True
        )
        advance(rest_movers, 2)
        attended, log_totals = attend_forward(packed)
        advance(rest_movers, 1)
        merged = lax.all_to_all(
            attended, "seq", split_axis=0, concat_axis=0, tiled=True
        ).reshape(D, local_rows)
        output, expand, reduce = split_weights(finish(rest_movers))
        weights.append((mixing, output, expand, reduce))
        if layer_index + 1 < LAYERS:
            following = layer_index + 1
            mixing_movers = mixing_gathers(mixing_weight[following], 1)
            rest_movers = later_weights(
                output_weight[following], expand_weight[following], reduce_weight[following]
            )
            merged = hold(merged, mixing_movers + rest_movers)
            advance(mixing_movers, 5)
            advance(rest_movers, 1)
        middle = hidden + (product("it,id->td", merged, output) + out_bias_all[layer_index])
        normed_two = layer_norm(middle, gains[1], shifts[1]).astype(jnp.bfloat16)
        pre_gelu = (
            jnp.concatenate([product("td,df->tf", normed_two, half) for half in expand], axis=1)
            + exp_bias_all[layer_index]
        )
        activated = gelu_tanh(pre_gelu).astype(jnp.bfloat16)
        saved.append((hidden, normed, packed, log_totals, merged, middle, normed_two, pre_gelu, activated))
        hidden = middle + (product("tf,fd->td", activated, reduce) + red_bias_all[layer_index])
    out_tokens = hidden.astype(jnp.bfloat16)

    running_grad = cotangent.astype(jnp.float32)
    large = [None] * LAYERS
    small_grads = [None] * LAYERS
    previous = []
    for layer_index in reversed(range(LAYERS)):
        layer_input, normed, packed, log_totals, merged, middle, normed_two, pre_gelu, activated = saved[
            layer_index
        ]
        mixing, output, expand, reduce = weights[layer_index]
        gains = gains_all[layer_index]
        shifts = shifts_all[layer_index]
        reduce_bias_grad = jnp.sum(running_grad, axis=0)
        grad_low = running_grad.astype(jnp.bfloat16)
        reduce_mover = ScatterSum(product("tf,td->fd", activated, grad_low), 1)
        reduce_mover.step()
        act_grad = product("td,fd->tf", grad_low, reduce)
        unused_value, gelu_pull = jax.vjp(gelu_tanh, pre_gelu)
        pre_grad = gelu_pull(act_grad)[0].astype(jnp.bfloat16)
        expand_bias_grad = jnp.sum(pre_grad.astype(jnp.float32), axis=0)
        advance(previous, 1)
        reduce_mover.step()
        expand_movers = [ScatterSum(product("td,tf->df", normed_two, pre_grad), 2)]
        advance(expand_movers, 1)
        half = pre_grad.shape[1] // 2
        halves = (pre_grad[:, :half], pre_grad[:, half:])
        second_in = product("tf,df->td", halves[0], expand[0]) + product(
            "tf,df->td", halves[1], expand[1]
        )
        unused_norm, norm_pull = jax.vjp(layer_norm, middle, gains[1], shifts[1])
        middle_grad, gain_two, shift_two = norm_pull(second_in)
        running_grad = running_grad + middle_grad
        output_bias_grad = jnp.sum(running_grad, axis=0)
        out_low = running_grad.astype(jnp.bfloat16)
        finish(previous)
        output_mover = ScatterSum(product("it,td->id", merged, out_low), 0)
        output_mover.step()
        movers = [reduce_mover] + expand_movers + [output_mover]
        merged_grad = product("td,id->it", out_low, output).astype(jnp.bfloat16)
        head_grad = lax.all_to_all(
            merged_grad.reshape(parts, heads, HD, local_rows),
            "seq",
            split_axis=0,
            concat_axis=0,
            tiled=True,
        )
        advance(movers, 2)
        packed_grad = attend_backward(packed, head_grad, log_totals)
        advance(movers, 1)
        mixed_grad = lax.all_to_all(
            packed_grad, "seq", split_axis=0, concat_axis=0, tiled=True
        )
        grad_thirds = [mixed_grad[:, n].reshape(D, local_rows) for n in range(3)]
        if layer_index:
            all_thirds = jnp.concatenate(grad_thirds, axis=0)
            mixing_movers = [ScatterSum(product("td,ct->dc", normed, all_thirds), 0)]
        else:
            mixing_movers = [
                ScatterSum(product("td,ct->dc", normed, grad_thirds[n]), n) for n in range(3)
            ]
        advance(mixing_movers, 2)
        mixing_bias_grad = jnp.stack(
            [jnp.sum(grad_thirds[n].astype(jnp.float32), axis=1) for n in (0, 2)]
        )
        first_in = sum(product("ct,dc->td", grad_thirds[n], mixing[n]) for n in range(3))
        unused_first, first_pull = jax.vjp(layer_norm, layer_input, gains[0], shifts[0])
        input_part, gain_one, shift_one = first_pull(first_in)
        running_grad = running_grad + input_part
        finish(movers)
        previous = mixing_movers
        large[layer_index] = (mixing_movers, [output_mover], expand_movers, [reduce_mover])
        small_grads[layer_index] = (
            jnp.stack([gain_one, gain_two]),
            jnp.stack([shift_one, shift_two]),
            mixing_bias_grad,
            output_bias_grad,
            expand_bias_grad,
            reduce_bias_grad,
        )

    rows = []
    for n, member in enumerate(small_members):
        both = jnp.stack([small_grads[index][n] for index in range(LAYERS)])
        both = both.reshape(both.shape[:-1] + (devices, -1))
        rows.append(jnp.moveaxis(both, -2, 0).reshape(devices, -1))
    packed_rows = jnp.concatenate(rows, axis=1)
    packed_rows = jnp.pad(packed_rows, ((0, 0), (0, slots - packed_rows.shape[1])))
    small_sum = ScatterSum(packed_rows.reshape(-1, 128), 0, jnp.float32)
    sums = finish(previous + [small_sum])[-1].reshape(-1)
    shards = []
    start = 0
    for member in small_members:
        shards.append(sums[start : start + member.size].reshape(member.shape))
        start += member.size
    gain_out, shift_out, mix_bias_out, out_bias_out, exp_bias_out, red_bias_out = shards
    mixing_out, output_out, expand_out, reduce_out = (
        jnp.stack(
            [
                jnp.concatenate([mover.result() for mover in large[index][n]], axis=1)
                for index in range(LAYERS)
            ]
        )
        for n in range(4)
    )
    return (
        out_tokens,
        running_grad,
        gain_out,
        shift_out,
        mixing_out,
        mix_bias_out,
        output_out,
        out_bias_out,
        expand_out,
        exp_bias_out,
        reduce_out,
        red_bias_out,
    )


def solution(mesh):
    return jax.shard_map(
        body,
        mesh=mesh,
        in_specs=(
            P(("dp", "seq"), None),
            P(("dp", "seq"), None),
            P(None, None, ("dp", "seq")),
            P(None, None, ("dp", "seq")),
            P(None, ("dp", "seq"), None),
            P(None, None, ("dp", "seq")),
            P(None, ("dp", "seq"), None),
            P(None, ("dp", "seq")),
            P(None, ("dp", "seq"), None),
            P(None, ("dp", "seq")),
            P(None, ("dp", "seq"), None),
            P(None, ("dp", "seq")),
        ),
        out_specs=(
            P(("dp", "seq"), None),
            P(("dp", "seq"), None),
            P(None, None, ("dp", "seq")),
            P(None, None, ("dp", "seq")),
            P(None, ("dp", "seq"), None),
            P(None, None, ("dp", "seq")),
            P(None, ("dp", "seq"), None),
            P(None, ("dp", "seq")),
            P(None, ("dp", "seq"), None),
            P(None, ("dp", "seq")),
            P(None, ("dp", "seq"), None),
            P(None, ("dp", "seq")),
        ),
        check_vma=False,
    )
```
